256 devices in a mesh: local: 8 (over z), node: 16 (over x, y), dp: 2 (over core).
Axes of the slice: x: 4, y: 4, z: 8, core: 2. Of those that a mesh axis runs over, the one named last changes fastest.
Arguments:
- tokens: bfloat16 [4096, 7168], P(('node', 'dp'), 'local'), may hold values from -6 to 6
- grad_out: bfloat16 [4096, 7168], P(('node', 'dp'), 'local'), may hold values from -6 to 6
- experts_of_token: int32 [4096, 4], P(('node', 'dp')), may hold values from 0 to 15, all different within a row; in each aligned block of 128 rows (0 to 127, 128 to 255, ...) at most 48 rows name the same one
- gate_weights: float32 [4096, 4], P(('node', 'dp')), may hold values from 0.05 to 0.6
- w_gate: bfloat16 [16, 7168, 1024], P('node', 'local'), may hold values from -0.0625 to 0.0625
- w_up: bfloat16 [16, 7168, 1024], P('node', 'local'), may hold values from -0.0625 to 0.0625
- w_down: bfloat16 [16, 1024, 7168], P('node', None, 'local'), may hold values from -0.1875 to 0.1875
Outputs:
- grad_tokens: bfloat16 [4096, 7168], P(('node', 'dp'), 'local')
- grad_gate: bfloat16 [16, 7168, 1024], P('node', ('local', 'dp'))
- grad_up: bfloat16 [16, 7168, 1024], P('node', ('local', 'dp'))
- grad_down: bfloat16 [16, 1024, 7168], P('node', None, ('local', 'dp'))
The draws below stay inside these ranges and needn't reach their ends.
Inputs may be any that keep to these rules, and one draw needn't show every extreme that they name: `experts_of_token`: in each aligned block of 128 rows (the tokens of one index of node and dp taken together) no expert is named by more than 48 rows, a bound that some block reaches; each row names 4 different experts.
All inputs are finite; a program needn't handle non-finite values.
Results may differ from the reference program's by a relative error of at most 0.03.
Values may be sent and summed in bfloat16 or wider, within the bound.
No kernel may reach another device: no remote copies, remote signals or barrier semaphores. Data moves between devices by JAX's collectives and lax.ppermute only.
A program may use at most 64 MiB of HBM per device.

```python
import math
import jax
import jax.numpy as jnp
import numpy as np
from jax import lax

D = 7168
HID = 1024
TOP = 4
TOK_DEV = 128
EXPERTS = 16
CAP = 48
TOKENS = 4096
N_LOCAL = 8
N_DP = 2


def block_scale(stream_key, dims, cuts, smallest, top_value):
    loudness = 1.0
    for position, blocks in cuts:
        steps = jax.random.uniform(jax.random.fold_in(jax.random.fold_in(stream_key, 6), position), (blocks,), jnp.float32, smallest / len(cuts), top_value / len(cuts))
        loudness = loudness * jnp.repeat(jnp.exp(steps), dims[position] // blocks).reshape((-1,) + (1,) * (len(dims) - 1 - position))
    return loudness


def shared_out(stream_key, own, number, rows, count, top, most, lean):
    order = jax.random.permutation(stream_key, count)
    heavy_load, common = shares(count, rows * top, most, lean, True), shares(count, rows * top, most, lean, False)
    places = jnp.arange(count)

    def named(lengths, rotation):
        used = int((lengths > 0).sum())
        fixed = max(1, used // 4)
        passed = fixed + (places - fixed + rotation * (used - fixed)) % max(1, count - fixed)
        return jnp.zeros((count,), jnp.int32).at[order[jnp.where(places < fixed, places, passed)]].set(jnp.asarray(lengths, jnp.int32))

    lengths = jnp.where(number % 4 == 0, named(heavy_load, number // 4), named(common, number - number // 4 - 1))
    mixed = jax.random.permutation(jax.random.fold_in(own, 3), count)
    donor, sink = mixed[0:count // 2 * 2:2], mixed[1:count // 2 * 2:2]
    slack = jnp.minimum(lengths[donor] - 1, most - lengths[sink]) // 2
    slack = jnp.where((donor == order[0]) | (sink == order[0]) | (lengths[sink] == 0), 0, jnp.maximum(slack, 0))
    passed = jax.random.randint(jax.random.fold_in(own, 4), (count // 2,), 0, 1 << 20) % (slack + 1)
    lengths = lengths.at[donor].add(-passed).at[sink].add(passed)
    labels = jnp.searchsorted(jnp.cumsum(lengths), jnp.arange(rows * top), side="right").astype(jnp.int32)
    listing = labels.reshape(top, rows).T
    listing = listing[jax.random.permutation(jax.random.fold_in(own, 1), rows)]
    rotation = jax.random.randint(jax.random.fold_in(own, 2), (rows, 1), 0, top)
    return jnp.take_along_axis(listing, (jnp.arange(top)[None, :] + rotation) % top, axis=1)


def shares(count, total, bound, skew, full):
    weights = [(1 << 20) // math.isqrt(rank ** skew) + 1 for rank in range(1, count + 1)]
    largest = bound if full else min(bound, max(-(-total // count), total * weights[0] // sum(weights)))
    least = 1 if total - largest >= count - 1 else 0
    counts, surplus = [largest] + [least] * (count - 1), total - largest - least * (count - 1)
    while surplus > 0:
        candidates = [i for i in range(1, count) if counts[i] < largest] or [i for i in range(1, count) if counts[i] < bound]
        pool, budget = sum([weights[i] for i in candidates]), surplus
        for i in candidates:
            addition = min(bound - counts[i], max(1, budget * weights[i] // pool), surplus)
            counts[i] = counts[i] + addition
            surplus = surplus - addition
    return np.array(counts)


def bell_draw(rng, extent, scale, reach, shards=(), kind=jnp.bfloat16):
    result = scale * jax.random.normal(rng, extent, jnp.float32)
    if shards:
        result = result * block_scale(rng, extent, shards, -0.22, 0.18)
    return jnp.clip(result, -reach, reach).astype(kind)


def setup_inputs(seed: int = 0) -> dict:
    keys = jax.random.split(jax.random.key(seed), 8)
    tokens = bell_draw(keys[0], (TOKENS, D), 1.0, 6.0, ((0, 32), (1, 8)))
    grad_out = bell_draw(keys[1], (TOKENS, D), 1.0, 6.0, ((0, 32), (1, 8)))
    experts_of_token_keys = jax.random.split(jax.random.fold_in(keys[2], 1), TOKENS // TOK_DEV)
    experts_of_token_turns = jax.random.permutation(jax.random.fold_in(keys[2], 3), TOKENS // TOK_DEV)
    experts_of_token = jax.vmap(lambda own, number: shared_out(jax.random.fold_in(keys[2], 2), own, number, TOK_DEV, EXPERTS, TOP, CAP, 2))(experts_of_token_keys, experts_of_token_turns).reshape((TOKENS, TOP))
    gate_weights = jnp.clip(0.05 + 0.55 * jax.random.uniform(keys[3], (TOKENS, TOP), jnp.float32) ** block_scale(keys[3], (TOKENS, TOP), ((0, 32),), -0.2, 0.2), 0.05, 0.6)
    w_gate = bell_draw(keys[4], (EXPERTS, D, HID), D ** -0.5, 0.0625, ((0, 16), (1, 8)))
    w_up = bell_draw(keys[5], (EXPERTS, D, HID), D ** -0.5, 0.0625, ((0, 16), (1, 8)))
    w_down = bell_draw(keys[6], (EXPERTS, HID, D), HID ** -0.5, 0.1875, ((0, 16), (2, 8)))
    return {"tokens": tokens, "grad_out": grad_out, "experts_of_token": experts_of_token, "gate_weights": gate_weights, "w_gate": w_gate, "w_up": w_up, "w_down": w_down}


def activate(pre_gate, pre_up, hidden_grad):
    sigma = jax.nn.sigmoid(pre_gate)
    swish = pre_gate * sigma
    hidden = (swish * pre_up).astype(jnp.bfloat16)
    grad_gate_pre = (hidden_grad * pre_up * sigma * (1.0 + pre_gate * (1.0 - sigma))).astype(jnp.bfloat16)
    grad_up_pre = (hidden_grad * swish).astype(jnp.bfloat16)
    return hidden, grad_gate_pre, grad_up_pre


def block_sum(left, right_blocks):
    block_width = D // N_LOCAL
    left_blocks = left.astype(jnp.float32).reshape(left.shape[0], N_LOCAL, block_width)
    parts = jnp.einsum("mld,ldh->lmh", left_blocks, right_blocks)
    rounded = lax.optimization_barrier(parts.astype(jnp.bfloat16)).astype(jnp.float32)
    return jnp.sum(rounded, axis=0)


def group_outer(left, right, group_of, filled):
    total = jnp.zeros((left.shape[1], right.shape[1]), jnp.float32)
    for group in range(N_DP):
        member = filled & (group_of == group)
        masked = jnp.where(member[:, None], left, jnp.zeros((), left.dtype))
        part = jnp.dot(masked.T, right, preferred_element_type=jnp.float32)
        total = total + lax.optimization_barrier(part.astype(jnp.bfloat16)).astype(jnp.float32)
    return total.astype(jnp.bfloat16)


def reference(tokens, grad_out, experts_of_token, gate_weights, w_gate, w_up, w_down):
    block_width = D // N_LOCAL
    assigned = TOKENS * TOP
    limit = (TOKENS // TOK_DEV) * CAP
    flat_ids = experts_of_token.reshape(-1)
    flat_gates = gate_weights.reshape(-1)

    def one_expert(carry, expert):
        picked = jnp.nonzero(flat_ids == expert, size=limit, fill_value=assigned)[0].astype(jnp.int32)
        filled = picked < assigned
        source = jnp.minimum(picked, assigned - 1)
        token_row = (source // TOP).astype(jnp.int32)
        group_of = ((token_row // TOK_DEV) % N_DP).astype(jnp.int32)
        rows_in = jnp.where(filled[:, None], tokens[token_row], jnp.zeros((), tokens.dtype))
        weight = jnp.where(filled, flat_gates[source], jnp.zeros((), flat_gates.dtype))
        rows_grad = (weight[:, None] * grad_out[token_row].astype(jnp.float32)).astype(jnp.bfloat16)
        gate_mat = w_gate[expert]
        up_mat = w_up[expert]
        down_mat = w_down[expert]
        pre_gate = block_sum(rows_in, gate_mat.astype(jnp.float32).reshape(N_LOCAL, block_width, HID))
        pre_up = block_sum(rows_in, up_mat.astype(jnp.float32).reshape(N_LOCAL, block_width, HID))
        down_blocks = jnp.transpose(down_mat.astype(jnp.float32).reshape(HID, N_LOCAL, block_width), (1, 2, 0))
        hidden_grad = block_sum(rows_grad, down_blocks)
        hidden, grad_gate_pre, grad_up_pre = activate(pre_gate, pre_up, hidden_grad)
        grad_down = group_outer(hidden, rows_grad, group_of, filled)
        grad_gate = group_outer(rows_in, grad_gate_pre, group_of, filled)
        grad_up = group_outer(rows_in, grad_up_pre, group_of, filled)
        expert_grad = (jnp.dot(grad_gate_pre, gate_mat.T, preferred_element_type=jnp.float32)
                       + jnp.dot(grad_up_pre, up_mat.T, preferred_element_type=jnp.float32)).astype(jnp.bfloat16)
        target = jnp.where(filled, token_row, TOKENS).astype(jnp.int32)
        carry = carry.at[target].add(expert_grad.astype(jnp.float32), mode="drop")
        return carry, (grad_gate, grad_up, grad_down)

    start = jnp.zeros((TOKENS, D), jnp.float32)
    total, stacked = lax.scan(one_expert, start, jnp.arange(EXPERTS, dtype=jnp.int32))
    return total.astype(jnp.bfloat16), stacked[0], stacked[1], stacked[2]
```

```python
import functools

import jax
import jax.numpy as jnp
from jax import lax
from jax.experimental import pallas as pl
from jax.experimental.pallas import tpu as pltpu
from jax.sharding import PartitionSpec as P

ORDER = "aa" + "ba" * 7 + "bb"
VMEM_LIMIT = 56 * 1024 * 1024
BF16 = jnp.bfloat16
F32 = jnp.float32


def activate(pre_gate, pre_up, hidden_grad):
    sigma = jax.nn.sigmoid(pre_gate)
    swish = pre_gate * sigma
    hidden = (swish * pre_up).astype(BF16)
    grad_gate_pre = (hidden_grad * pre_up * sigma * (1.0 + pre_gate * (1.0 - sigma))).astype(BF16)
    grad_up_pre = (hidden_grad * swish).astype(BF16)
    return (hidden, grad_gate_pre, grad_up_pre)


def dot_f32(left, right, left_dim, right_dim):
    return lax.dot_general(
        left,
        right,
        (((left_dim,), (right_dim,)), ((), ())),
        preferred_element_type=F32,
    )


def partials_kernel(x_ref, g_ref, gate_ref, up_ref, down_ref, out_ref, right_ref, left_ref):
    blocks = out_ref.shape[0]

    def put(i, left, right, right_dim=0):
        value = dot_f32(left[...], right[...], 1, right_dim).astype(BF16)
        out_ref[:, i] = value.reshape(blocks, -1, value.shape[1])

    put(0, x_ref, gate_ref)
    put(1, x_ref, up_ref)
    put(2, g_ref, down_ref, 1)

    @pl.when(pl.program_id(0) == 0)
    def _():
        right_ref[...] = out_ref[blocks // 2]

    @pl.when(pl.program_id(0) == 1)
    def _():
        left_ref[...] = out_ref[blocks // 2]


def partials(x, g, gate, up, down, blocks):
    rows, width = x.shape
    hid = gate.shape[1]
    tile = hid // 2
    whole = pl.BlockSpec((rows, width), lambda j: (0, 0))
    weight = pl.BlockSpec((width, tile), lambda j: (0, j))
    half = pl.BlockSpec((3, rows // blocks, tile), lambda j: (0, 0, 0))
    half_shape = jax.ShapeDtypeStruct((3, rows // blocks, tile), BF16)
    return pl.pallas_call(
        partials_kernel,
        grid=(2,),
        in_specs=[
            whole,
            whole,
            weight,
            weight,
            pl.BlockSpec((tile, width), lambda j: (j, 0)),
        ],
        out_specs=(
            pl.BlockSpec((blocks, 3, rows // blocks, tile), lambda j: (0, 0, 0, j)),
            half,
            half,
        ),
        out_shape=(
            jax.ShapeDtypeStruct((blocks, 3, rows // blocks, hid), BF16),
            half_shape,
            half_shape,
        ),
        compiler_params=pltpu.CompilerParams(vmem_limit_bytes=VMEM_LIMIT),
    )(x, g, gate, up, down)


def expert_grad_kernel(first, *refs):
    refs, (gate_ref, up_ref, out_ref, act_ref) = refs[:-4], refs[-4:]
    blocks = refs if first else refs[1:]
    start = 0 if first else refs[0].shape[1]
    rows = blocks[0].shape[1]
    end = start + len(blocks) * rows
    if not first:
        act_ref[:, :start, :] = refs[0][...]
    for k, block in enumerate(blocks):
        act_ref[:, start + k * rows : start + (k + 1) * rows, :] = block[...]
    out_ref[...] = (
        dot_f32(act_ref[1, start:end], gate_ref[...], 1, 1)
        + dot_f32(act_ref[2, start:end], up_ref[...], 1, 1)
    ).astype(BF16)


def expert_grads(earlier, blocks, gate, up):
    rows = len(blocks) * blocks[0].shape[1]
    width, hid = gate.shape
    start = sum(e.shape[1] for e in earlier)
    return pl.pallas_call(
        functools.partial(expert_grad_kernel, not earlier),
        out_shape=(
            jax.ShapeDtypeStruct((rows, width), BF16),
            jax.ShapeDtypeStruct((3, start + rows, hid), BF16),
        ),
        compiler_params=pltpu.CompilerParams(vmem_limit_bytes=VMEM_LIMIT),
    )(*earlier, *blocks, gate, up)


def shift(x, step):
    size = lax.axis_size("local")
    return lax.ppermute(x, "local", [(i, (i + step) % size) for i in range(size)])


def after(x, token):
    if token is None:
        return x
    return lax.optimization_barrier((x, token))[0]


def ring_reduce(part, right, left):
    size = part.shape[0]
    far = size // 2
    half = part.shape[-1] // 2
    for k in range(far - 1, -1, -1):
        token = yield (right, left)
        right, left = after((shift(right, 1), shift(left, -1)), token)
        right, left = right.astype(F32), left.astype(F32)
        if k == 0:
            return part[0].astype(F32) + right + left
        to_right, to_left = part[k].astype(F32), part[size - k].astype(F32)
        if k == far - 1:
            to_right = jnp.concatenate(
                [to_right[..., :half] + right, to_right[..., half:]], axis=-1
            )
            to_left = jnp.concatenate([to_left[..., :half], to_left[..., half:] + left], axis=-1)
        else:
            to_right, to_left = to_right + right, to_left + left
        right, left = to_right.astype(BF16), to_left.astype(BF16)


def ring_gather(block):
    size = lax.axis_size("local")
    far = size // 2
    half = block.shape[-1] // 2
    blocks = [block] * size
    right = left = block
    for k in range(1, far + 1):
        token = yield (right, left)
        right, left = after((shift(right, 1), shift(left, -1)), token)
        blocks[size - k], blocks[k] = right, left
        if k == far - 1:
            right, left = right[..., :half], left[..., half:]
    blocks[far] = jnp.concatenate([right, left], axis=-1)
    return blocks


def swap(x):
    return lax.ppermute(x, "dp", [(0, 1), (1, 0)])


def on_device(tokens, grad_out, experts_of_token, gate_weights, w_gate, w_up, w_down):
    rows, width = tokens.shape
    chosen = experts_of_token.shape[1]
    experts = lax.axis_size("node")
    size = lax.axis_size("local")
    capacity = min(rows, 3 * rows * chosen // (2 * experts))
    slots = capacity // len(set(ORDER))
    place = lax.axis_index("local")
    core = lax.axis_index("dp")
    gate_mat, up_mat, down_mat = w_gate[0], w_up[0], w_down[0]

    turn = experts // size
    turned = [
        [z * experts + (i + z * turn) % experts for i in range(experts)] for z in range(size)
    ]

    def exchange(x, groups):
        return lax.all_to_all(
            x,
            ("local", "node"),
            split_axis=0,
            concat_axis=0,
            axis_index_groups=groups,
            tiled=True,
        )

    expert = jnp.arange(experts, dtype=jnp.int32)

    def routing(expert):
        named = experts_of_token.T[:, None, :] == expert[None, :, None]
        member = jnp.any(named, axis=0)
        weight_of = jnp.sum(jnp.where(named, gate_weights.T[:, None, :], 0.0), axis=0)
        before = jnp.arange(rows)[:, None] < jnp.arange(rows)[None, :]
        rank = dot_f32(member.astype(BF16), before.astype(BF16), 1, 0)
        return jnp.where(member, rank, -1.0).astype(jnp.int32), weight_of

    def dispatch(expert, first, groups):
        rank, weight_of = routing(expert)
        slot = jnp.arange(first, first + slots, dtype=jnp.int32)
        select = rank[:, None, :] == slot[None, :, None]
        weight = jnp.sum(jnp.where(select, weight_of[:, None, :], 0.0), axis=2).reshape(-1, 1)
        select = select.astype(BF16).reshape(experts * slots, rows)
        rows_in = dot_f32(select, tokens, 1, 0).astype(BF16)
        rows_grad = (weight * dot_f32(select, grad_out, 1, 0)).astype(BF16)
        sent = jnp.concatenate(
            [rows_in.reshape(experts, slots, width), rows_grad.reshape(experts, slots, width)],
            axis=1,
        )
        got = exchange(sent, groups)
        return select, got[:, :slots].reshape(-1, width), got[:, slots:].reshape(-1, width)

    def halves(x):
        low, high = x[:, : width // 2], x[:, width // 2 :]
        return jnp.where(core == 0, low, high), jnp.where(core == 0, high, low)

    turned_expert = (expert + place * turn) % experts
    finished = {}

    def chain(name, first, earlier):
        select, x, g = dispatch(turned_expert, first, turned)
        token = yield None
        x, g = after((x, g), token)
        part, right, left = partials(x, g, gate_mat, up_mat, down_mat, size)
        pre = yield from ring_reduce(part, right, left)
        act = jnp.stack(activate(pre[0], pre[1], pre[2]))
        blocks = yield from ring_gather(act)
        earlier = [finished[e]["act"] for e in earlier]
        expert_grad, act = expert_grads(earlier, blocks, gate_mat, up_mat)
        back = exchange(expert_grad.reshape(experts, slots, width), turned)
        finished[name] = {"select": select, "x": x, "g": g, "act": act, "back": back}
        yield expert_grad

    names = sorted(set(ORDER))
    chains = {n: chain(n, i * slots, names[:i][-1:]) for i, n in enumerate(names)}
    for name in names:
        next(chains[name])
    token, back = None, None
    left = {name: ORDER.count(name) for name in names}
    for name in ORDER:
        left[name] -= 1
        if left[name] == 0 and back is not None:
            token = (token, back)
        token = chains[name].send(token)
        if left[name] == 0:
            back = finished[name]["back"]

    done = [finished[name] for name in names]
    x_own, x_other = halves(jnp.concatenate([f["x"] for f in done]))
    g_own, g_other = halves(jnp.concatenate([f["g"] for f in done]))
    act = done[-1]["act"]
    other = (
        swap(dot_f32(x_other, act[1], 0, 0).astype(BF16)),
        swap(dot_f32(x_other, act[2], 0, 0).astype(BF16)),
        swap(dot_f32(act[0], g_other, 0, 0).astype(BF16)),
    )
    own = (
        dot_f32(x_own, act[1], 0, 0),
        dot_f32(x_own, act[2], 0, 0),
        dot_f32(act[0], g_own, 0, 0),
    )
    grads = [(u + v.astype(F32)).astype(BF16)[None] for u, v in zip(own, other)]
    grad_tokens = sum(
        dot_f32(f["select"], f["back"].reshape(-1, width), 0, 0) for f in done
    )
    return (grad_tokens.astype(BF16), *grads)


def solution(mesh):
    in_specs = (
        P(("node", "dp"), "local"),
        P(("node", "dp"), "local"),
        P(("node", "dp"), None),
        P(("node", "dp"), None),
        P("node", "local", None),
        P("node", "local", None),
        P("node", None, "local"),
    )
    out_specs = (
        P(("node", "dp"), "local"),
        P("node", ("local", "dp"), None),
        P("node", ("local", "dp"), None),
        P("node", None, ("local", "dp")),
    )
    return jax.shard_map(
        on_device, mesh=mesh, in_specs=in_specs, out_specs=out_specs, check_vma=False
    )
```

```python
import functools

import jax
import jax.numpy as jnp
from jax import lax
from jax.experimental import pallas as pl
from jax.experimental.pallas import tpu as pltpu
from jax.sharding import PartitionSpec as P

ORDER = "aa" + "ba" * 7 + "bb"
VMEM_LIMIT = 20 * 1024 * 1024
VMEM_MOST = 56 * 1024 * 1024
BF16 = jnp.bfloat16
F32 = jnp.float32


def activate(pre_gate, pre_up, hidden_grad):
    sigma = jax.nn.sigmoid(pre_gate)
    swish = pre_gate * sigma
    hidden = (swish * pre_up).astype(BF16)
    grad_gate_pre = (hidden_grad * pre_up * sigma * (1.0 + pre_gate * (1.0 - sigma))).astype(BF16)
    grad_up_pre = (hidden_grad * swish).astype(BF16)
    return (hidden, grad_gate_pre, grad_up_pre)


def dot_f32(left, right, left_dim, right_dim):
    return lax.dot_general(
        left,
        right,
        (((left_dim,), (right_dim,)), ((), ())),
        preferred_element_type=F32,
    )


def partials_kernel(x_ref, g_ref, gate_ref, up_ref, down_ref, out_ref, right_ref, left_ref):
    blocks = out_ref.shape[0]

    def put(i, left, right, right_dim=0):
        value = dot_f32(left[...], right[...], 1, right_dim).astype(BF16)
        out_ref[:, i] = value.reshape(blocks, -1, value.shape[1])

    put(0, x_ref, gate_ref)
    put(1, x_ref, up_ref)
    put(2, g_ref, down_ref, 1)

    @pl.when(pl.program_id(0) == 0)
    def _():
        right_ref[...] = out_ref[blocks // 2]

    @pl.when(pl.program_id(0) == 1)
    def _():
        left_ref[...] = out_ref[blocks // 2]


def partials(x, g, gate, up, down, blocks):
    rows, width = x.shape
    hid = gate.shape[1]
    tile = hid // 2
    whole = pl.BlockSpec((rows, width), lambda j: (0, 0))
    weight = pl.BlockSpec((width, tile), lambda j: (0, j))
    half = pl.BlockSpec((3, rows // blocks, tile), lambda j: (0, 0, 0))
    half_shape = jax.ShapeDtypeStruct((3, rows // blocks, tile), BF16)
    return pl.pallas_call(
        partials_kernel,
        grid=(2,),
        in_specs=[
            whole,
            whole,
            weight,
            weight,
            pl.BlockSpec((tile, width), lambda j: (j, 0)),
        ],
        out_specs=(
            pl.BlockSpec((blocks, 3, rows // blocks, tile), lambda j: (0, 0, 0, j)),
            half,
            half,
        ),
        out_shape=(
            jax.ShapeDtypeStruct((blocks, 3, rows // blocks, hid), BF16),
            half_shape,
            half_shape,
        ),
        compiler_params=pltpu.CompilerParams(vmem_limit_bytes=VMEM_LIMIT),
    )(x, g, gate, up, down)


def absorb_kernel(count, places, *refs):
    blocks, (gate_ref, up_ref) = refs[:count], refs[count : count + 2]
    grad_ref, made_ref, sems = refs[-3:]
    gate_grad = jnp.concatenate([block[1] for block in blocks])
    up_grad = jnp.concatenate([block[2] for block in blocks])
    made = dot_f32(gate_grad, gate_ref[...], 1, 1) + dot_f32(up_grad, up_ref[...], 1, 1)
    made_ref[...] = made.astype(BF16).reshape(made_ref.shape)
    copies = [
        pltpu.make_async_copy(made_ref.at[i], grad_ref.at[k], sems.at[i])
        for i, k in enumerate(places)
    ]
    for copy in copies:
        copy.start()
    for copy in copies:
        copy.wait()


def absorb(blocks, places, size, gate, up, grad):
    count, rows = len(blocks), blocks[0].shape[1]
    width = gate.shape[0]
    carried = [] if grad is None else [grad]
    whole = pl.BlockSpec(memory_space=pltpu.VMEM)
    in_hbm = pl.BlockSpec(memory_space=pltpu.HBM)
    return pl.pallas_call(
        functools.partial(absorb_kernel, count, places),
        in_specs=[whole] * (count + 2) + [in_hbm] * len(carried),
        out_specs=in_hbm,
        out_shape=jax.ShapeDtypeStruct((size, rows, width), BF16),
        scratch_shapes=[
            pltpu.VMEM((count, rows, width), BF16),
            pltpu.SemaphoreType.DMA((count,)),
        ],
        input_output_aliases={count + 2: 0} if carried else {},
        compiler_params=pltpu.CompilerParams(vmem_limit_bytes=VMEM_LIMIT),
    )(*blocks, gate, up, *carried)


def weight_grads_kernel(chains, count, *refs):
    x_refs, g_refs = refs[:chains], refs[chains : 2 * chains]
    blocks = refs[2 * chains : 2 * chains + count]
    rest = refs[2 * chains + count :]
    step = pl.program_id(0)
    act = jnp.concatenate([block[0] for block in blocks])

    def put(i, parts):
        grad = dot_f32(jnp.concatenate([part[...] for part in parts]), act, 0, 0)
        if len(rest) == 1:
            rest[0][0] = grad.astype(BF16)
        else:
            rest[1 + i][...] = (grad + rest[0][0].astype(F32)).astype(BF16)

    for i, parts in enumerate((g_refs, x_refs, x_refs)):
        pl.when(step == i)(functools.partial(put, i, parts))


def weight_grads(x, g, blocks, added):
    width = x[0].shape[1]
    _, rows, hid = blocks[0].shape
    part = pl.BlockSpec(x[0].shape, lambda i: (0, 0))
    each = pl.BlockSpec((1, width, hid), lambda i: (i, 0, 0))
    if added is None:
        out_specs, out_shape = each, jax.ShapeDtypeStruct((3, width, hid), BF16)
    else:
        out_specs = [pl.BlockSpec((width, hid), lambda i: (0, 0))] * 3
        out_shape = [jax.ShapeDtypeStruct((width, hid), BF16)] * 3
    return pl.pallas_call(
        functools.partial(weight_grads_kernel, len(x), len(blocks)),
        grid=(3,),
        in_specs=[part] * (2 * len(x))
        + [pl.BlockSpec((1, rows, hid), lambda i: (i, 0, 0))] * len(blocks)
        + ([] if added is None else [each]),
        out_specs=out_specs,
        out_shape=out_shape,
        compiler_params=pltpu.CompilerParams(vmem_limit_bytes=VMEM_MOST),
    )(*x, *g, *blocks, *([] if added is None else [added]))


def shift(x, step):
    size = lax.axis_size("local")
    return lax.ppermute(x, "local", [(i, (i + step) % size) for i in range(size)])


def after(x, token):
    if token is None:
        return x
    return lax.optimization_barrier((x, token))[0]


def ring_reduce(part, right, left, aside):
    size = part.shape[0]
    far = size // 2
    half = part.shape[-1] // 2
    for k in range(far - 1, -1, -1):
        token = yield (right, left)
        if k == 1:
            token = (token, aside)
        right, left = after((shift(right, 1), shift(left, -1)), token)
        right, left = right.astype(F32), left.astype(F32)
        if k == 0:
            return part[0].astype(F32) + right + left
        to_right, to_left = part[k].astype(F32), part[size - k].astype(F32)
        if k == far - 1:
            to_right = jnp.concatenate(
                [to_right[..., :half] + right, to_right[..., half:]], axis=-1
            )
            to_left = jnp.concatenate([to_left[..., :half], to_left[..., half:] + left], axis=-1)
        else:
            to_right, to_left = to_right + right, to_left + left
        right, left = to_right.astype(BF16), to_left.astype(BF16)


def ring_gather(block, take):
    size = lax.axis_size("local")
    far = size // 2
    half = block.shape[-1] // 2
    right = left = block
    ready = ([block], [0])
    for k in range(1, far + 1):
        token = yield (right, left)
        taken = take(*ready)
        right, left = after((shift(right, 1), shift(left, -1)), (token, taken))
        ready = ([left, right], [k, size - k])
        if k == far - 1:
            right, left = right[..., :half], left[..., half:]
    take([jnp.concatenate([right, left], axis=-1)], [far])


def swap(x):
    return lax.ppermute(x, "dp", [(0, 1), (1, 0)])


def on_device(tokens, grad_out, experts_of_token, gate_weights, w_gate, w_up, w_down):
    rows, width = tokens.shape
    chosen = experts_of_token.shape[1]
    experts = lax.axis_size("node")
    size = lax.axis_size("local")
    capacity = min(rows, 3 * rows * chosen // (2 * experts))
    slots = capacity // len(set(ORDER))
    place = lax.axis_index("local")
    core = lax.axis_index("dp")
    gate_mat, up_mat, down_mat = w_gate[0], w_up[0], w_down[0]

    turn = experts // size
    turned = [
        [z * experts + (i + z * turn) % experts for i in range(experts)] for z in range(size)
    ]

    def exchange(x, groups):
        return lax.all_to_all(
            x,
            ("local", "node"),
            split_axis=0,
            concat_axis=0,
            axis_index_groups=groups,
            tiled=True,
        )

    expert = jnp.arange(experts, dtype=jnp.int32)

    def routing(expert):
        named = experts_of_token.T[:, None, :] == expert[None, :, None]
        member = jnp.any(named, axis=0)
        weight_of = jnp.sum(jnp.where(named, gate_weights.T[:, None, :], 0.0), axis=0)
        before = jnp.arange(rows)[:, None] < jnp.arange(rows)[None, :]
        rank = dot_f32(member.astype(BF16), before.astype(BF16), 1, 0)
        return jnp.where(member, rank, -1.0).astype(jnp.int32), weight_of

    def dispatch(expert, first, groups):
        rank, weight_of = routing(expert)
        slot = jnp.arange(first, first + slots, dtype=jnp.int32)
        select = rank[:, None, :] == slot[None, :, None]
        weight = jnp.sum(jnp.where(select, weight_of[:, None, :], 0.0), axis=2).reshape(-1, 1)
        select = select.astype(BF16).reshape(experts * slots, rows)
        rows_in = dot_f32(select, tokens, 1, 0).astype(BF16)
        rows_grad = (weight * dot_f32(select, grad_out, 1, 0)).astype(BF16)
        sent = jnp.concatenate(
            [rows_in.reshape(experts, slots, width), rows_grad.reshape(experts, slots, width)],
            axis=1,
        )
        got = exchange(sent, groups)
        return select, got[:, :slots].reshape(-1, width), got[:, slots:].reshape(-1, width)

    def halves(x):
        low, high = x[:, : width // 2], x[:, width // 2 :]
        return jnp.where(core == 0, low, high), jnp.where(core == 0, high, low)

    turned_expert = (expert + place * turn) % experts
    finished = {}

    def chain(name, number):
        select, x, g = dispatch(turned_expert, number * slots, turned)
        token = yield None
        x, g = after((x, g), token)
        part, right, left = partials(x, g, gate_mat, up_mat, down_mat, size)
        halved = halves(x), halves(g)
        pre = yield from ring_reduce(part, right, left, halved)
        grad = None

        blocks = [None] * size

        def take(got, places):
            nonlocal grad
            grad = absorb(got, places, size, gate_mat, up_mat, grad)
            for block, k in zip(got, places):
                blocks[k] = block
            return grad

        yield from ring_gather(jnp.stack(activate(pre[0], pre[1], pre[2])), take)
        back = exchange(grad.reshape(experts, slots, width), turned)
        finished[name] = {
            "select": select,
            "x": halved[0],
            "g": halved[1],
            "blocks": blocks,
            "grad": grad,
            "back": back,
        }
        yield grad

    names = sorted(set(ORDER))
    chains = {n: chain(n, i) for i, n in enumerate(names)}
    for name in names:
        next(chains[name])
    token, back = None, None
    left = {name: ORDER.count(name) for name in names}
    for name in ORDER:
        left[name] -= 1
        if left[name] == 0 and back is not None:
            token = (token, back)
        token = chains[name].send(token)
        if left[name] == 0:
            back = finished[name]["back"]

    done = [finished[name] for name in names]
    x_own, x_other = zip(*(f["x"] for f in done))
    g_own, g_other = zip(*(f["g"] for f in done))
    blocks = [block for f in done for block in f["blocks"]]
    blocks = after(blocks, done[-1]["grad"])
    received = swap(weight_grads(x_other, g_other, blocks, None))
    down, gate, up = weight_grads(x_own, g_own, blocks, received)
    backs = after([f["back"] for f in done], (down, gate, up))
    grad_tokens = sum(
        dot_f32(f["select"], back.reshape(-1, width), 0, 0) for f, back in zip(done, backs)
    )
    return (grad_tokens.astype(BF16), gate[None], up[None], down.T[None])


def solution(mesh):
    in_specs = (
        P(("node", "dp"), "local"),
        P(("node", "dp"), "local"),
        P(("node", "dp"), None),
        P(("node", "dp"), None),
        P("node", "local", None),
        P("node", "local", None),
        P("node", None, "local"),
    )
    out_specs = (
        P(("node", "dp"), "local"),
        P("node", ("local", "dp"), None),
        P("node", ("local", "dp"), None),
        P("node", None, ("local", "dp")),
    )
    return jax.shard_map(
        on_device, mesh=mesh, in_specs=in_specs, out_specs=out_specs, check_vma=False
    )
```

```python
import functools

import jax
import jax.numpy as jnp
from jax import lax
from jax.experimental import pallas as pl
from jax.experimental.pallas import tpu as pltpu
from jax.sharding import PartitionSpec as P

ORDER = "aa" + "ba" * 7 + "bb"
VMEM_LIMIT = 20 * 1024 * 1024
VMEM_MOST = 56 * 1024 * 1024
BF16 = jnp.bfloat16
F32 = jnp.float32


def activate(pre_gate, pre_up, hidden_grad):
    sigma = jax.nn.sigmoid(pre_gate)
    swish = pre_gate * sigma
    hidden = (swish * pre_up).astype(BF16)
    grad_gate_pre = (hidden_grad * pre_up * sigma * (1.0 + pre_gate * (1.0 - sigma))).astype(BF16)
    grad_up_pre = (hidden_grad * swish).astype(BF16)
    return (hidden, grad_gate_pre, grad_up_pre)


def dot_f32(left, right, left_dim, right_dim):
    return lax.dot_general(
        left,
        right,
        (((left_dim,), (right_dim,)), ((), ())),
        preferred_element_type=F32,
    )


def partials_kernel(x_ref, g_ref, gate_ref, up_ref, down_ref, out_ref, right_ref, left_ref):
    blocks = out_ref.shape[0]

    def put(i, left, right, right_dim=0):
        value = dot_f32(left[...], right[...], 1, right_dim).astype(BF16)
        out_ref[:, i] = value.reshape(blocks, -1, value.shape[1])

    put(0, x_ref, gate_ref)
    put(1, x_ref, up_ref)
    put(2, g_ref, down_ref, 1)

    @pl.when(pl.program_id(0) == 0)
    def _():
        right_ref[...] = out_ref[blocks // 2]

    @pl.when(pl.program_id(0) == 1)
    def _():
        left_ref[...] = out_ref[blocks // 2]


def partials(x, g, gate, up, down, blocks):
    rows, width = x.shape
    hid = gate.shape[1]
    tile = hid // 2
    whole = pl.BlockSpec((rows, width), lambda j: (0, 0))
    weight = pl.BlockSpec((width, tile), lambda j: (0, j))
    half = pl.BlockSpec((3, rows // blocks, tile), lambda j: (0, 0, 0))
    half_shape = jax.ShapeDtypeStruct((3, rows // blocks, tile), BF16)
    return pl.pallas_call(
        partials_kernel,
        grid=(2,),
        in_specs=[
            whole,
            whole,
            weight,
            weight,
            pl.BlockSpec((tile, width), lambda j: (j, 0)),
        ],
        out_specs=(
            pl.BlockSpec((blocks, 3, rows // blocks, tile), lambda j: (0, 0, 0, j)),
            half,
            half,
        ),
        out_shape=(
            jax.ShapeDtypeStruct((blocks, 3, rows // blocks, hid), BF16),
            half_shape,
            half_shape,
        ),
        compiler_params=pltpu.CompilerParams(vmem_limit_bytes=VMEM_MOST),
    )(x, g, gate, up, down)


def absorb_kernel(count, places, number, *refs):
    blocks, (gate_ref, up_ref) = refs[:count], refs[count : count + 2]
    grad_ref, made_ref, sems = refs[-3:]
    gate_grad = jnp.concatenate([block[1] for block in blocks])
    up_grad = jnp.concatenate([block[2] for block in blocks])
    made = dot_f32(gate_grad, gate_ref[...], 1, 1) + dot_f32(up_grad, up_ref[...], 1, 1)
    made_ref[...] = made.reshape(made_ref.shape).astype(BF16)
    nodes = made_ref.shape[1]
    copies = [
        pltpu.make_async_copy(
            made_ref.at[i], grad_ref.at[pl.ds(k * nodes, nodes), number], sems.at[i]
        )
        for i, k in enumerate(places)
    ]
    for copy in copies:
        copy.start()
    for copy in copies:
        copy.wait()


def absorb(blocks, places, number, shape, gate, up, grad):
    count, rows = len(blocks), blocks[0].shape[1]
    _, _, slots, width = shape
    carried = [] if grad is None else [grad]
    whole = pl.BlockSpec(memory_space=pltpu.VMEM)
    in_hbm = pl.BlockSpec(memory_space=pltpu.HBM)
    return pl.pallas_call(
        functools.partial(absorb_kernel, count, places, number),
        in_specs=[whole] * (count + 2) + [in_hbm] * len(carried),
        out_specs=in_hbm,
        out_shape=jax.ShapeDtypeStruct(shape, BF16),
        scratch_shapes=[
            pltpu.VMEM((count, rows // slots, slots, width), BF16),
            pltpu.SemaphoreType.DMA((count,)),
        ],
        input_output_aliases={count + 2: 0} if carried else {},
        compiler_params=pltpu.CompilerParams(vmem_limit_bytes=VMEM_LIMIT),
    )(*blocks, gate, up, *carried)


def weight_grads_kernel(chains, count, *refs):
    x_refs, g_refs = refs[:chains], refs[chains : 2 * chains]
    blocks = refs[2 * chains : 2 * chains + count]
    rest = refs[2 * chains + count :]
    step = pl.program_id(0)
    act = jnp.concatenate([block[0] for block in blocks])

    def put(i, parts):
        grad = dot_f32(jnp.concatenate([part[...] for part in parts]), act, 0, 0)
        if len(rest) == 1:
            rest[0][0] = grad.astype(BF16)
        else:
            rest[1 + i][...] = (grad + rest[0][0].astype(F32)).astype(BF16)

    for i, parts in enumerate((g_refs, x_refs, x_refs)):
        pl.when(step == i)(functools.partial(put, i, parts))


def weight_grads(x, g, blocks, added):
    width = x[0].shape[1]
    _, rows, hid = blocks[0].shape
    part = pl.BlockSpec(x[0].shape, lambda i: (0, 0))
    each = pl.BlockSpec((1, width, hid), lambda i: (i, 0, 0))
    if added is None:
        out_specs, out_shape = each, jax.ShapeDtypeStruct((3, width, hid), BF16)
    else:
        out_specs = [pl.BlockSpec((width, hid), lambda i: (0, 0))] * 3
        out_shape = [jax.ShapeDtypeStruct((width, hid), BF16)] * 3
    return pl.pallas_call(
        functools.partial(weight_grads_kernel, len(x), len(blocks)),
        grid=(3,),
        in_specs=[part] * (2 * len(x))
        + [pl.BlockSpec((1, rows, hid), lambda i: (i, 0, 0))] * len(blocks)
        + ([] if added is None else [each]),
        out_specs=out_specs,
        out_shape=out_shape,
        compiler_params=pltpu.CompilerParams(vmem_limit_bytes=VMEM_MOST),
    )(*x, *g, *blocks, *([] if added is None else [added]))


def shift(x, step):
    size = lax.axis_size("local")
    return lax.ppermute(x, "local", [(i, (i + step) % size) for i in range(size)])


def after(x, token):
    if token is None:
        return x
    return lax.optimization_barrier((x, token))[0]


def ring_reduce(part, right, left, aside):
    size = part.shape[0]
    far = size // 2
    half = part.shape[-1] // 2
    for k in range(far - 1, -1, -1):
        token = yield (right, left)
        if k == 1:
            token = (token, aside)
        right, left = after((shift(right, 1), shift(left, -1)), token)
        right, left = right.astype(F32), left.astype(F32)
        if k == 0:
            return part[0].astype(F32) + right + left
        to_right, to_left = part[k].astype(F32), part[size - k].astype(F32)
        if k == far - 1:
            to_right = jnp.concatenate(
                [to_right[..., :half] + right, to_right[..., half:]], axis=-1
            )
            to_left = jnp.concatenate([to_left[..., :half], to_left[..., half:] + left], axis=-1)
        else:
            to_right, to_left = to_right + right, to_left + left
        right, left = to_right.astype(BF16), to_left.astype(BF16)


def ring_gather(block, take):
    size = lax.axis_size("local")
    far = size // 2
    half = block.shape[-1] // 2
    right = left = block
    ready = ([block], [0])
    for k in range(1, far + 1):
        token = yield (right, left)
        taken = take(*ready)
        right, left = after((shift(right, 1), shift(left, -1)), (token, taken))
        ready = ([left, right], [k, size - k])
        if k == far - 1:
            right, left = right[..., :half], left[..., half:]
    take([jnp.concatenate([right, left], axis=-1)], [far])


def swap(x):
    return lax.ppermute(x, "dp", [(0, 1), (1, 0)])


def on_device(tokens, grad_out, experts_of_token, gate_weights, w_gate, w_up, w_down):
    rows, width = tokens.shape
    chosen = experts_of_token.shape[1]
    experts = lax.axis_size("node")
    size = lax.axis_size("local")
    capacity = min(rows, 3 * rows * chosen // (2 * experts))
    slots = capacity // len(set(ORDER))
    place = lax.axis_index("local")
    core = lax.axis_index("dp")
    gate_mat, up_mat, down_mat = w_gate[0], w_up[0], w_down[0]

    turn = experts // size
    turned = [
        [z * experts + (i + z * turn) % experts for i in range(experts)] for z in range(size)
    ]

    def exchange(x, groups):
        return lax.all_to_all(
            x,
            ("local", "node"),
            split_axis=0,
            concat_axis=0,
            axis_index_groups=groups,
            tiled=True,
        )

    expert = jnp.arange(experts, dtype=jnp.int32)

    def routing(expert):
        named = experts_of_token.T[:, None, :] == expert[None, :, None]
        member = jnp.any(named, axis=0)
        weight_of = jnp.sum(jnp.where(named, gate_weights.T[:, None, :], 0.0), axis=0)
        before = jnp.arange(rows)[:, None] < jnp.arange(rows)[None, :]
        rank = dot_f32(member.astype(BF16), before.astype(BF16), 1, 0)
        return jnp.where(member, rank, -1.0).astype(jnp.int32), weight_of

    def select_slots(rank, first, slots):
        slot = jnp.arange(first, first + slots, dtype=jnp.int32)
        return rank[:, None, :] == slot[None, :, None]

    def dispatch(expert, first, groups):
        rank, weight_of = routing(expert)
        select = select_slots(rank, first, slots)
        weight = jnp.sum(jnp.where(select, weight_of[:, None, :], 0.0), axis=2).reshape(-1, 1)
        select = select.astype(BF16).reshape(experts * slots, rows)
        rows_in = dot_f32(select, tokens, 1, 0).astype(BF16)
        rows_grad = (weight * dot_f32(select, grad_out, 1, 0)).astype(BF16)
        sent = jnp.concatenate(
            [rows_in.reshape(experts, slots, width), rows_grad.reshape(experts, slots, width)],
            axis=1,
        )
        got = exchange(sent, groups)
        return got[:, :slots].reshape(-1, width), got[:, slots:].reshape(-1, width)

    def halves(x):
        low, high = x[:, : width // 2], x[:, width // 2 :]
        return jnp.where(core == 0, low, high), jnp.where(core == 0, high, low)

    turned_expert = (expert + place * turn) % experts
    finished = {}
    state = {"grad": None}

    def chain(name, number):
        x, g = dispatch(turned_expert, number * slots, turned)
        token = yield None
        x, g = after((x, g), token)
        part, right, left = partials(x, g, gate_mat, up_mat, down_mat, size)
        halved = halves(x), halves(g)
        pre = yield from ring_reduce(part, right, left, halved)
        blocks = [None] * size

        def take(got, places):
            state["grad"] = absorb(
                got,
                places,
                number,
                (experts, len(names), slots, width),
                gate_mat,
                up_mat,
                state["grad"],
            )
            for block, k in zip(got, places):
                blocks[k] = block
            return state["grad"]

        yield from ring_gather(jnp.stack(activate(pre[0], pre[1], pre[2])), take)
        finished[name] = {"x": halved[0], "g": halved[1], "blocks": blocks}
        yield state["grad"]

    names = sorted(set(ORDER))
    chains = {n: chain(n, i) for i, n in enumerate(names)}
    for name in names:
        next(chains[name])
    token = None
    for name in ORDER:
        token = chains[name].send(token)

    done = [finished[name] for name in names]
    x_own, x_other = zip(*(f["x"] for f in done))
    g_own, g_other = zip(*(f["g"] for f in done))
    blocks = [block for f in done for block in f["blocks"]]
    back = exchange(state["grad"], turned)
    blocks = after(blocks, state["grad"])
    received = swap(weight_grads(x_other, g_other, blocks, None))
    down, gate, up = weight_grads(x_own, g_own, blocks, received)
    back = after(back, (down, gate, up)).reshape(-1, width)
    select = select_slots(routing(turned_expert)[0], 0, capacity).astype(BF16)
    grad_tokens = dot_f32(select.reshape(-1, rows), back, 0, 0)
    return (grad_tokens.astype(BF16), gate[None], up[None], down.T[None])


def solution(mesh):
    in_specs = (
        P(("node", "dp"), "local"),
        P(("node", "dp"), "local"),
        P(("node", "dp"), None),
        P(("node", "dp"), None),
        P("node", "local", None),
        P("node", "local", None),
        P("node", None, "local"),
    )
    out_specs = (
        P(("node", "dp"), "local"),
        P("node", ("local", "dp"), None),
        P("node", ("local", "dp"), None),
        P("node", None, ("local", "dp")),
    )
    return jax.shard_map(
        on_device, mesh=mesh, in_specs=in_specs, out_specs=out_specs, check_vma=False
    )
```

```python
import functools

import jax
import jax.numpy as jnp
from jax import lax
from jax.experimental import pallas as pl
from jax.experimental.pallas import tpu as pltpu
from jax.sharding import PartitionSpec as P

ORDER = "aa" + "ba" * 7 + "bb"
VMEM_LIMIT = 20 * 1024 * 1024
VMEM_MOST = 56 * 1024 * 1024
BF16 = jnp.bfloat16
F32 = jnp.float32


def activate(pre_gate, pre_up, hidden_grad):
    sigma = jax.nn.sigmoid(pre_gate)
    swish = pre_gate * sigma
    hidden = (swish * pre_up).astype(BF16)
    grad_gate_pre = (hidden_grad * pre_up * sigma * (1.0 + pre_gate * (1.0 - sigma))).astype(BF16)
    grad_up_pre = (hidden_grad * swish).astype(BF16)
    return (hidden, grad_gate_pre, grad_up_pre)


def dot_f32(left, right, left_dim, right_dim):
    return lax.dot_general(
        left,
        right,
        (((left_dim,), (right_dim,)), ((), ())),
        preferred_element_type=F32,
    )


def partials_kernel(x_ref, g_ref, gate_ref, up_ref, down_ref, out_ref, right_ref, left_ref):
    blocks = out_ref.shape[0]

    def put(i, left, right, right_dim=0):
        value = dot_f32(left[...], right[...], 1, right_dim).astype(BF16)
        out_ref[:, i] = value.reshape(blocks, -1, value.shape[1])

    put(0, x_ref, gate_ref)
    put(1, x_ref, up_ref)
    put(2, g_ref, down_ref, 1)

    @pl.when(pl.program_id(0) == 0)
    def _():
        right_ref[...] = out_ref[blocks // 2]

    @pl.when(pl.program_id(0) == 1)
    def _():
        left_ref[...] = out_ref[blocks // 2]


def partials(x, g, gate, up, down, blocks):
    rows, width = x.shape
    hid = gate.shape[1]
    tile = hid // 2
    whole = pl.BlockSpec((rows, width), lambda j: (0, 0))
    weight = pl.BlockSpec((width, tile), lambda j: (0, j))
    half = pl.BlockSpec((3, rows // blocks, tile), lambda j: (0, 0, 0))
    half_shape = jax.ShapeDtypeStruct((3, rows // blocks, tile), BF16)
    return pl.pallas_call(
        partials_kernel,
        grid=(2,),
        in_specs=[
            whole,
            whole,
            weight,
            weight,
            pl.BlockSpec((tile, width), lambda j: (j, 0)),
        ],
        out_specs=(
            pl.BlockSpec((blocks, 3, rows // blocks, tile), lambda j: (0, 0, 0, j)),
            half,
            half,
        ),
        out_shape=(
            jax.ShapeDtypeStruct((blocks, 3, rows // blocks, hid), BF16),
            half_shape,
            half_shape,
        ),
        compiler_params=pltpu.CompilerParams(vmem_limit_bytes=VMEM_MOST),
    )(x, g, gate, up, down)


def absorb_kernel(count, places, number, *refs):
    blocks, (gate_ref, up_ref) = refs[:count], refs[count : count + 2]
    grad_ref, made_ref, sems = refs[-3:]
    gate_grad = jnp.concatenate([block[1] for block in blocks])
    up_grad = jnp.concatenate([block[2] for block in blocks])
    made = dot_f32(gate_grad, gate_ref[...], 1, 1) + dot_f32(up_grad, up_ref[...], 1, 1)
    made_ref[...] = made.reshape(made_ref.shape).astype(BF16)
    nodes = made_ref.shape[1]
    copies = [
        pltpu.make_async_copy(
            made_ref.at[i], grad_ref.at[pl.ds(k * nodes, nodes), number], sems.at[i]
        )
        for i, k in enumerate(places)
    ]
    for copy in copies:
        copy.start()
    for copy in copies:
        copy.wait()


def absorb(blocks, places, number, shape, gate, up, grad):
    count, rows = len(blocks), blocks[0].shape[1]
    _, _, slots, width = shape
    carried = [] if grad is None else [grad]
    whole = pl.BlockSpec(memory_space=pltpu.VMEM)
    in_hbm = pl.BlockSpec(memory_space=pltpu.HBM)
    return pl.pallas_call(
        functools.partial(absorb_kernel, count, places, number),
        in_specs=[whole] * (count + 2) + [in_hbm] * len(carried),
        out_specs=in_hbm,
        out_shape=jax.ShapeDtypeStruct(shape, BF16),
        scratch_shapes=[
            pltpu.VMEM((count, rows // slots, slots, width), BF16),
            pltpu.SemaphoreType.DMA((count,)),
        ],
        input_output_aliases={count + 2: 0} if carried else {},
        compiler_params=pltpu.CompilerParams(vmem_limit_bytes=VMEM_LIMIT),
    )(*blocks, gate, up, *carried)


def weight_grads_kernel(chains, count, *refs):
    x_refs, g_refs = refs[:chains], refs[chains : 2 * chains]
    blocks = refs[2 * chains : 2 * chains + count]
    rest = refs[2 * chains + count :]
    step = pl.program_id(0)
    act = jnp.concatenate([block[0] for block in blocks])

    def put(i, parts):
        grad = dot_f32(jnp.concatenate([part[...] for part in parts]), act, 0, 0)
        if len(rest) == 1:
            rest[0][0] = grad.astype(BF16)
        else:
            rest[1 + i][...] = (grad + rest[0][0].astype(F32)).astype(BF16)

    for i, parts in enumerate((g_refs, x_refs, x_refs)):
        pl.when(step == i)(functools.partial(put, i, parts))


def weight_grads(x, g, blocks, added):
    width = x[0].shape[1]
    _, rows, hid = blocks[0].shape
    part = pl.BlockSpec(x[0].shape, lambda i: (0, 0))
    each = pl.BlockSpec((1, width, hid), lambda i: (i, 0, 0))
    if added is None:
        out_specs, out_shape = each, jax.ShapeDtypeStruct((3, width, hid), BF16)
    else:
        out_specs = [pl.BlockSpec((width, hid), lambda i: (0, 0))] * 3
        out_shape = [jax.ShapeDtypeStruct((width, hid), BF16)] * 3
    return pl.pallas_call(
        functools.partial(weight_grads_kernel, len(x), len(blocks)),
        grid=(3,),
        in_specs=[part] * (2 * len(x))
        + [pl.BlockSpec((1, rows, hid), lambda i: (i, 0, 0))] * len(blocks)
        + ([] if added is None else [each]),
        out_specs=out_specs,
        out_shape=out_shape,
        compiler_params=pltpu.CompilerParams(vmem_limit_bytes=VMEM_MOST),
    )(*x, *g, *blocks, *([] if added is None else [added]))


def shift(x, step):
    size = lax.axis_size("local")
    return lax.ppermute(x, "local", [(i, (i + step) % size) for i in range(size)])


def after(x, token):
    if token is None:
        return x
    return lax.optimization_barrier((x, token))[0]


def ring_reduce(part, right, left, aside):
    size = part.shape[0]
    far = size // 2
    half = part.shape[-1] // 2
    for k in range(far - 1, -1, -1):
        token = yield (right, left)
        if k == 1:
            token = (token, aside)
        right, left = after((shift(right, 1), shift(left, -1)), token)
        right, left = right.astype(F32), left.astype(F32)
        if k == 0:
            return part[0].astype(F32) + right + left
        to_right, to_left = part[k].astype(F32), part[size - k].astype(F32)
        if k == far - 1:
            to_right = jnp.concatenate(
                [to_right[..., :half] + right, to_right[..., half:]], axis=-1
            )
            to_left = jnp.concatenate([to_left[..., :half], to_left[..., half:] + left], axis=-1)
        else:
            to_right, to_left = to_right + right, to_left + left
        right, left = to_right.astype(BF16), to_left.astype(BF16)


def ring_gather(block, take):
    size = lax.axis_size("local")
    far = size // 2
    half = block.shape[-1] // 2
    right = left = block
    ready = ([block], [0])
    for k in range(1, far + 1):
        token = yield (right, left)
        taken = take(*ready)
        right, left = after((shift(right, 1), shift(left, -1)), (token, taken))
        ready = ([left, right], [k, size - k])
        if k == far - 1:
            right, left = right[..., :half], left[..., half:]
    take([jnp.concatenate([right, left], axis=-1)], [far])


def swap(x):
    return lax.ppermute(x, "dp", [(0, 1), (1, 0)])


def on_device(tokens, grad_out, experts_of_token, gate_weights, w_gate, w_up, w_down):
    rows, width = tokens.shape
    chosen = experts_of_token.shape[1]
    experts = lax.axis_size("node")
    size = lax.axis_size("local")
    capacity = min(rows, 3 * rows * chosen // (2 * experts))
    slots = capacity // len(set(ORDER))
    place = lax.axis_index("local")
    core = lax.axis_index("dp")
    gate_mat, up_mat, down_mat = w_gate[0], w_up[0], w_down[0]

    turn = experts // size
    turned = [
        [z * experts + (i + z * turn) % experts for i in range(experts)] for z in range(size)
    ]

    def exchange(x, groups):
        return lax.all_to_all(
            x,
            ("local", "node"),
            split_axis=0,
            concat_axis=0,
            axis_index_groups=groups,
            tiled=True,
        )

    expert = jnp.arange(experts, dtype=jnp.int32)

    def routing(expert):
        named = experts_of_token.T[:, None, :] == expert[None, :, None]
        member = jnp.any(named, axis=0)
        weight_of = jnp.sum(jnp.where(named, gate_weights.T[:, None, :], 0.0), axis=0)
        before = jnp.arange(rows)[:, None] < jnp.arange(rows)[None, :]
        rank = dot_f32(member.astype(BF16), before.astype(BF16), 1, 0)
        return jnp.where(member, rank, -1.0).astype(jnp.int32), weight_of

    def select_slots(rank, first, slots):
        slot = jnp.arange(first, first + slots, dtype=jnp.int32)
        return rank[:, None, :] == slot[None, :, None]

    def dispatch(expert, first, groups):
        rank, weight_of = routing(expert)
        select = select_slots(rank, first, slots)
        weight = jnp.sum(jnp.where(select, weight_of[:, None, :], 0.0), axis=2).reshape(-1, 1)
        select = select.astype(BF16).reshape(experts * slots, rows)
        rows_in = dot_f32(select, tokens, 1, 0).astype(BF16)
        rows_grad = (weight * dot_f32(select, grad_out, 1, 0)).astype(BF16)
        sent = jnp.concatenate(
            [rows_in.reshape(experts, slots, width), rows_grad.reshape(experts, slots, width)],
            axis=1,
        )
        got = exchange(sent, groups)
        return got[:, :slots].reshape(-1, width), got[:, slots:].reshape(-1, width)

    def halves(x):
        low, high = x[:, : width // 2], x[:, width // 2 :]
        return jnp.where(core == 0, low, high), jnp.where(core == 0, high, low)

    turned_expert = (expert + place * turn) % experts
    finished = {}
    state = {"grad": None}

    def chain(name, number):
        x, g = dispatch(turned_expert, number * slots, turned)
        token = yield None
        x, g = after((x, g), token)
        part, right, left = partials(x, g, gate_mat, up_mat, down_mat, size)
        halved = halves(x), halves(g)
        pre = yield from ring_reduce(part, right, left, halved)
        blocks = [None] * size

        def take(got, places):
            state["grad"] = absorb(
                got,
                places,
                number,
                (experts, len(names), slots, width),
                gate_mat,
                up_mat,
                state["grad"],
            )
            for block, k in zip(got, places):
                blocks[k] = block
            return state["grad"]

        yield from ring_gather(jnp.stack(activate(pre[0], pre[1], pre[2])), take)
        finished[name] = {"x": halved[0], "g": halved[1], "blocks": blocks}
        yield None

    names = sorted(set(ORDER))
    chains = {n: chain(n, i) for i, n in enumerate(names)}
    for name in names:
        next(chains[name])
    token = None
    for name in ORDER:
        token = chains[name].send(token)

    done = [finished[name] for name in names]
    x_own, x_other = zip(*(f["x"] for f in done))
    g_own, g_other = zip(*(f["g"] for f in done))
    blocks = [block for f in done for block in f["blocks"]]
    back = exchange(state["grad"], turned)
    blocks = after(blocks, state["grad"])
    received = swap(weight_grads(x_other, g_other, blocks, None))
    down, gate, up = weight_grads(x_own, g_own, blocks, received)
    back = after(back, (down, gate, up)).reshape(-1, width)
    select = select_slots(routing(turned_expert)[0], 0, capacity).astype(BF16)
    grad_tokens = dot_f32(select.reshape(-1, rows), back, 0, 0)
    return (grad_tokens.astype(BF16), gate[None], up[None], down.T[None])


def solution(mesh):
    in_specs = (
        P(("node", "dp"), "local"),
        P(("node", "dp"), "local"),
        P(("node", "dp"), None),
        P(("node", "dp"), None),
        P("node", "local", None),
        P("node", "local", None),
        P("node", None, "local"),
    )
    out_specs = (
        P(("node", "dp"), "local"),
        P("node", ("local", "dp"), None),
        P("node", ("local", "dp"), None),
        P("node", None, ("local", "dp")),
    )
    return jax.shard_map(
        on_device, mesh=mesh, in_specs=in_specs, out_specs=out_specs, check_vma=False
    )
```
